32 devices in a mesh: seq: 8 (over y, x, core), tp: 4 (over z).
Axes of the slice: x: 2, y: 2, z: 4, core: 2. Of those that a mesh axis runs over, the one named last changes fastest.
Arguments:
- residual: bfloat16 [4096, 2048], P('seq', 'tp'), may hold values from -6 to 6
- norm_gain: float32 [2048], replicated, may hold values from 0.3 to 3
- query_weight: bfloat16 [2048, 1024], P(None, 'tp'), as said below
- key_weight: bfloat16 [2048, 1024], P(None, 'tp'), as said below
- value_weight: bfloat16 [2048, 1024], P(None, 'tp'), may hold values from -0.375 to 0.375
- out_weight: bfloat16 [1024, 2048], P('tp'), may hold values from -0.1875 to 0.1875
- segment_start: int32 [4096], P('seq'), may hold values from 0 to 3968, as said below
- token_valid: int32 [4096], P('seq'), may hold values from 0 to 1, as said below
- page_slot: int32 [32], P('seq'), may hold values from 4 to 63, as said below
Outputs:
- hidden: bfloat16 [4096, 2048], P('seq', 'tp')
- cache: bfloat16 [64, 128, 2048], P('seq', None, 'tp')
The draws below stay inside these ranges and needn't reach their ends.
Inputs may be any that keep to these rules, and one draw needn't show every extreme that they name: `segment_start`: prompts start at multiples of 128 and are contiguous; each holds at most 2048 tokens and one holds exactly 2048. `token_valid`: zeros form a tail of the last page of a prompt; the first token of every prompt is 1. No two pages share a cache page; page_slot // 8 is the device that holds the page's tokens, or the next device when that one holds tokens of the same prompt. `query_weight`: independent entries whose scale falls as the inverse square root of 2048. `key_weight`: independent entries whose scale falls as the inverse square root of 2048.
All inputs are finite; a program needn't handle non-finite values.
Results may differ from the reference program's by a relative error of at most 0.02.
The reference program's roundings to bfloat16 on the way count: a program that leaves them out, or rounds other values in their place, can miss the bound.
Values may be sent and summed in bfloat16 or wider, within the bound.
A program may use at most 128 MiB of HBM per device.

```python
import math
import jax
import jax.numpy as jnp
from jax import lax

D = 2048
HEADS = 16
HD = 64
PAGE = 128
TOKENS = 4096
TILES = 32
TILES_DEV = 4
SLOT_DEV = 8
SLOTS = 64
LONGEST = 2048


def shuffled(key, device_count):
    scores = jax.random.randint(key, (device_count, TILES_DEV), 0, 1 << 20)
    scores = scores * TILES_DEV + jnp.arange(TILES_DEV, dtype=jnp.int32)[None, :]
    return jnp.argsort(scores, axis=1).astype(jnp.int32)


def layout(key):
    tile_count = TILES
    longest_tiles = LONGEST // PAGE
    group_key = jax.random.fold_in(key, 11)
    bit_key = jax.random.fold_in(key, 12)
    pad_key = jax.random.fold_in(key, 13)
    place_key = jax.random.fold_in(key, 14)
    move_key = jax.random.fold_in(key, 15)
    shift_key = jax.random.fold_in(key, 16)
    keep_key = jax.random.fold_in(key, 17)
    moved_key = jax.random.fold_in(key, 18)
    tile_ids = jnp.arange(tile_count, dtype=jnp.int32)
    shift = jax.random.randint(shift_key, (), 1, longest_tiles)
    relative = tile_ids - shift
    window_of = jnp.floor_divide(relative, longest_tiles)
    inside = relative - window_of * longest_tiles
    windows = (tile_count - shift) // longest_tiles
    chosen = jax.random.randint(place_key, (), 0, windows)
    exponent = jax.random.randint(group_key, (tile_count // 8 + 1,), 0, 7)
    period = jnp.repeat(jnp.left_shift(jnp.int32(1), exponent), 8)[:tile_count]
    random_bits = jax.random.randint(bit_key, (tile_count,), 0, 1 << 20)
    starts = random_bits % period == 0
    on_grid = inside == 0
    outside_flags = starts | on_grid | (tile_ids == tile_count - 1) | (tile_ids == 0)
    starts = jnp.where(window_of == chosen, on_grid, outside_flags)
    start_tile = lax.cummax(jnp.where(starts, tile_ids, 0))
    seg_ends = jnp.concatenate([starts[1:], jnp.ones((1,), dtype=bool)])
    last_tile = lax.cummin(jnp.where(seg_ends, tile_ids, tile_count), reverse=True)
    padding = jax.random.randint(pad_key, (tile_count,), 0, PAGE)
    in_row = jnp.arange(PAGE, dtype=jnp.int32)
    validity = jnp.logical_not(seg_ends[:, None] & (in_row[None, :] >= PAGE - padding[:, None]))
    segment_ids = jnp.repeat(start_tile * PAGE, PAGE)
    owner_dev = tile_ids // TILES_DEV
    within = tile_ids % TILES_DEV
    device_count = tile_count // TILES_DEV
    keep_order = shuffled(keep_key, device_count)
    moved_order = shuffled(moved_key, device_count)
    keep_place = keep_order[owner_dev, within]
    moved_place = moved_order[owner_dev, within]
    can_move = (owner_dev + 1) * TILES_DEV <= last_tile
    move_next = jax.random.randint(move_key, (tile_count,), 0, 2) * can_move.astype(jnp.int32)
    slots = jnp.where(move_next > 0, (owner_dev + 1) * SLOT_DEV + moved_place, owner_dev * SLOT_DEV + TILES_DEV + keep_place)
    return (segment_ids.astype(jnp.int32), validity.reshape(-1).astype(jnp.int32), slots.astype(jnp.int32))


def draw_segment_start(key, part):
    return layout(key)[0]


def draw_token_valid(key, part):
    return layout(key)[1]


def draw_page_slot(key, part):
    return layout(key)[2]


def projection(key):
    base = jnp.clip(jax.random.normal(key, (D, HEADS * HD), jnp.float32), -4.0, 4.0) * D ** (-0.5)
    return base.astype(jnp.bfloat16)


def draw_query_weight(key, part):
    return projection(jax.random.fold_in(key, 21))


def draw_key_weight(key, part):
    return projection(jax.random.fold_in(key, 22))


def block_levels(key, dims, pieces, low, high):
    level, own = 1.0, jax.random.fold_in(key, 6)
    for dim, shards_of in pieces:
        heights = jnp.exp(jax.random.uniform(jax.random.fold_in(own, dim), (shards_of,), jnp.float32, low / len(pieces), high / len(pieces)))
        level = level * jnp.repeat(heights, dims[dim] // shards_of).reshape([-1 if axis == dim else 1 for axis in range(len(dims))])
    return level


def scatter_about(own_key, shape, deviation, most, cuts=(), kind=jnp.bfloat16):
    result = deviation * jax.random.normal(own_key, shape, jnp.float32)
    if cuts:
        result = result * block_levels(own_key, shape, cuts, -0.22, 0.18)
    return jnp.clip(result, -most, most).astype(kind)


def setup_inputs(seed: int = 0) -> dict:
    arg_keys = jax.random.split(jax.random.key(seed), 10)
    residual = scatter_about(arg_keys[0], (TOKENS, D), 0.5, 6.0, ((0, 8), (1, 4)))
    norm_gain = jnp.clip(jnp.exp(jax.random.uniform(arg_keys[1], (D,), jnp.float32, math.log(0.3), math.log(3.0))), 0.3, 3.0)
    query_weight = draw_query_weight(jax.random.fold_in(arg_keys[9], 71), 0)
    key_weight = draw_key_weight(jax.random.fold_in(arg_keys[9], 71), 0)
    value_weight = scatter_about(arg_keys[4], (D, HEADS * HD), (D // 9) ** -0.5, 0.375, ((1, 4),))
    out_weight = scatter_about(arg_keys[5], (HEADS * HD, D), (HEADS * HD) ** -0.5, 0.1875, ((0, 4),))
    segment_start = draw_segment_start(jax.random.fold_in(arg_keys[9], 71), 0)
    token_valid = draw_token_valid(jax.random.fold_in(arg_keys[9], 71), 0)
    page_slot = draw_page_slot(jax.random.fold_in(arg_keys[9], 71), 0)
    return {"residual": residual, "norm_gain": norm_gain, "query_weight": query_weight, "key_weight": key_weight, "value_weight": value_weight, "out_weight": out_weight, "segment_start": segment_start, "token_valid": token_valid, "page_slot": page_slot}


THETA = 130000.0
EPS = 1e-05

def rotate(inputs, positions):
    half_dim = inputs.shape[-1] // 2
    frequency = THETA ** (-2.0 * jnp.arange(half_dim, dtype=jnp.float32) / inputs.shape[-1])
    angles = positions.astype(jnp.float32)[:, None] * frequency[None, :]
    cosine = jnp.cos(angles)[:, None, :]
    sine_part = jnp.sin(angles)[:, None, :]
    front_half = inputs[..., :half_dim]
    back_half = inputs[..., half_dim:]
    return jnp.concatenate([front_half * cosine - back_half * sine_part, back_half * cosine + front_half * sine_part], axis=-1)

def reference(residual, norm_gain, query_weight, key_weight, value_weight, out_weight, segment_start, token_valid, page_slot):
    token_count = residual.shape[0]
    head_count = query_weight.shape[1] // HD
    widened = residual.astype(jnp.float32)
    mean_sq = lax.optimization_barrier(jnp.mean(widened * widened, axis=1, keepdims=True))
    normed = (widened * lax.rsqrt(mean_sq + EPS) * norm_gain[None, :]).astype(jnp.bfloat16)
    places = jnp.arange(token_count, dtype=jnp.int32)
    offsets = places - segment_start
    queries = jnp.dot(normed, query_weight, preferred_element_type=jnp.float32).reshape(token_count, head_count, HD)
    key_raw = jnp.dot(normed, key_weight, preferred_element_type=jnp.float32).reshape(token_count, head_count, HD)
    value_raw = jnp.dot(normed, value_weight, preferred_element_type=jnp.float32).reshape(token_count, head_count, HD)
    query_rot = lax.optimization_barrier(rotate(queries, offsets).astype(jnp.bfloat16))
    key_rot = lax.optimization_barrier(rotate(key_raw, offsets).astype(jnp.bfloat16))
    values = lax.optimization_barrier(value_raw.astype(jnp.bfloat16))
    key_group = jnp.where(token_valid > 0, segment_start, -1)
    query_block = min(512, token_count)
    window = min(LONGEST + query_block, token_count)
    score_scale = HD ** (-0.5)

    def attend(block_index):
        block_start = block_index * query_block
        key_begin = jnp.clip(block_start + query_block - window, 0, token_count - window).astype(jnp.int32)
        query_part = lax.dynamic_slice_in_dim(query_rot, block_start, query_block, 0).astype(jnp.float32)
        key_part = lax.dynamic_slice_in_dim(key_rot, key_begin, window, 0).astype(jnp.float32)
        value_part = lax.dynamic_slice_in_dim(values, key_begin, window, 0).astype(jnp.float32)
        query_seg = lax.dynamic_slice_in_dim(segment_start, block_start, query_block, 0)
        key_seg = lax.dynamic_slice_in_dim(key_group, key_begin, window, 0)
        query_pos = block_start + jnp.arange(query_block, dtype=jnp.int32)
        key_pos = key_begin + jnp.arange(window, dtype=jnp.int32)
        allowed = (key_seg[None, :] == query_seg[:, None]) & (key_pos[None, :] <= query_pos[:, None])
        scores = jnp.einsum('qhd,khd->hqk', query_part, key_part, precision=lax.Precision.HIGHEST) * score_scale
        masked = jnp.where(allowed[None], scores, -1e+30)
        row_max = lax.optimization_barrier(jnp.max(masked, axis=2, keepdims=True))
        weights = jnp.where(allowed[None], jnp.exp(masked - row_max), 0.0)
        denominator = lax.optimization_barrier(jnp.sum(weights, axis=2))
        rounded = lax.optimization_barrier(weights.astype(jnp.bfloat16)).astype(jnp.float32)
        mixed = jnp.einsum('hqk,khd->qhd', rounded, value_part, precision=lax.Precision.HIGHEST)
        mixed = mixed / jnp.transpose(denominator)[:, :, None]
        return mixed.astype(jnp.bfloat16)
    attended = lax.map(attend, jnp.arange(token_count // query_block, dtype=jnp.int32))
    attended = attended.reshape(token_count, head_count * HD)
    projected = jnp.dot(attended, out_weight, preferred_element_type=jnp.float32)
    hidden = (widened + projected).astype(jnp.bfloat16)
    cache_rows = jnp.concatenate([key_rot[:, :, None, :], values[:, :, None, :]], axis=2).reshape(token_count, head_count * 2 * HD)
    cache_rows = jnp.where(token_valid[:, None] > 0, cache_rows, jnp.zeros_like(cache_rows))
    destination = page_slot[places // PAGE] * PAGE + places % PAGE
    cache = jnp.zeros((SLOTS * PAGE, head_count * 2 * HD), jnp.bfloat16).at[destination].set(cache_rows)
    return (hidden, cache.reshape(SLOTS, PAGE, head_count * 2 * HD))
```

```python
import functools

import jax
import jax.numpy as jnp
from jax import lax
from jax.experimental import pallas as pl
from jax.experimental.pallas import tpu as pltpu
from jax.sharding import PartitionSpec as P

HD = 64
PAGE = 128
SPAN = 16
THETA = 130000.0
EPS = 1e-05
MESH = pl.DeviceIdType.MESH
F32 = jnp.float32
BF16 = jnp.bfloat16


def kernel(
    S, T, R, G,
    res_ref, gain_ref, wq_ref, wk_ref, wv_ref, wo_ref, cos_ref, sin_ref, seg_ref, valid_ref, meta_ref,
    hid_ref, cache_ref,
    gath, nbuf, qpad, kv, meta, att, wo_all, bias,
    z_recv, zl_send, zr_send, wo_send, wo_recv, bc_send, bc_recv, meta_send, meta_recv,
    kv_send, kv_recv, sib_send, att_send, att_recv,
):
    i = lax.axis_index("seq")
    t = lax.axis_index("tp")
    rows_all, width = res_ref.shape
    C = rows_all // PAGE
    HL = wq_ref.shape[1] // HD
    core = lax.rem(i, 2)
    sib = i + 1 - 2 * core
    g = lax.rem(i, G)
    base = i - g
    wrows = wo_ref.shape[0] // G

    far = max(R, G - 1)
    barrier = pltpu.get_barrier_semaphore()
    for d in range(1, far + 1):
        @pl.when(i + d < S)
        def _(d=d):
            pl.semaphore_signal(barrier, inc=1, device_id=(i + d, t), device_id_type=MESH)

        @pl.when(i - d >= 0)
        def _(d=d):
            pl.semaphore_signal(barrier, inc=1, device_id=(i - d, t), device_id_type=MESH)
    for k in range(1, T):
        pl.semaphore_signal(barrier, inc=1, device_id=(i, lax.rem(t + k, T)), device_id_type=MESH)
    pl.semaphore_wait(barrier, jnp.minimum(i, far) + jnp.minimum(S - 1 - i, far) + (T - 1))

    def rows_of(c):
        return pl.ds(pl.multiple_of(c * PAGE, PAGE), PAGE)

    def wo_copy(s, to):
        r = pl.ds(pl.multiple_of(g * wrows, wrows), wrows)
        return pltpu.make_async_remote_copy(
            src_ref=wo_ref.at[r, pl.ds(pl.multiple_of(to * width, width), width)],
            dst_ref=wo_all.at[s, r, :],
            send_sem=wo_send.at[to], recv_sem=wo_recv.at[s],
            device_id=(i, to), device_id_type=MESH)

    def bc_copy(owner, to):
        r = pl.ds(pl.multiple_of(owner * wrows, wrows), wrows)
        return pltpu.make_async_remote_copy(
            src_ref=wo_all.at[:, r, :], dst_ref=wo_all.at[:, r, :],
            send_sem=bc_send.at[to], recv_sem=bc_recv.at[owner],
            device_id=(base + to, t), device_id_type=MESH)

    def meta_copy(d):
        return pltpu.make_async_remote_copy(
            src_ref=meta_ref, dst_ref=meta.at[d - 1],
            send_sem=meta_send.at[d - 1], recv_sem=meta_recv.at[d - 1],
            device_id=(i + d, t), device_id_type=MESH)

    def z_copy(s, c, step, own):
        r = rows_of(c)
        sems = zr_send if step > 0 else zl_send
        return pltpu.make_async_remote_copy(
            src_ref=res_ref.at[r, :] if own else gath.at[s, r, :],
            dst_ref=gath.at[s, r, :],
            send_sem=sems.at[s, c], recv_sem=z_recv.at[s, c],
            device_id=(i, t + step), device_id_type=MESH)

    def kv_copy(d, c):
        r = rows_of(c)
        return pltpu.make_async_remote_copy(
            src_ref=kv.at[0, r, :], dst_ref=kv.at[d, r, :],
            send_sem=kv_send.at[d, c], recv_sem=kv_recv.at[d, c],
            device_id=(i + d, t), device_id_type=MESH)

    def sib_copy(src, dst, c):
        r = rows_of(c)
        return pltpu.make_async_remote_copy(
            src_ref=kv.at[src, r, :], dst_ref=kv.at[dst, r, :],
            send_sem=sib_send.at[dst, c], recv_sem=kv_recv.at[dst, c],
            device_id=(sib, t), device_id_type=MESH)

    def att_copy(s, to, c):
        r = rows_of(c)
        return pltpu.make_async_remote_copy(
            src_ref=att.at[s, r, :], dst_ref=att.at[s, r, :],
            send_sem=att_send.at[to, c], recv_sem=att_recv.at[s, c],
            device_id=(i, to), device_id_type=MESH)

    def send_own(c):
        @pl.when(t + 1 < T)
        def _():
            z_copy(t, c, 1, True).start()

        @pl.when(t >= 1)
        def _():
            z_copy(t, c, -1, True).start()

    send_own(0)
    for k in range(1, T):
        wo_copy(t, lax.rem(t + k, T)).start()
    if C > 1:
        send_own(1)
    for d in range(1, R + 1):
        @pl.when(i + d < S)
        def _(d=d):
            meta_copy(d).start()

    gath[t] = res_ref[...]
    mine = pl.ds(pl.multiple_of(g * wrows, wrows), wrows)
    wo_all[t, mine, :] = wo_ref[mine, pl.ds(pl.multiple_of(t * width, width), width)]
    for d in range(1, R + 1):
        @pl.when(i < d)
        def _(d=d):
            kv[d] = jnp.zeros(kv.shape[1:], BF16)
            meta[d - 1] = jnp.full(meta.shape[1:], -1, jnp.int32)

    lane128 = lax.broadcasted_iota(jnp.int32, (PAGE, 128), 1)
    low = lane128 < HD
    first = lax.rem(lane128, HD) < HD // 2

    def rotated(x, cs, sn):
        fwd = pltpu.roll(x, 128 - HD // 2, 1)
        back = pltpu.roll(x, HD // 2, 1)
        return x * cs + jnp.where(first, fwd, back) * sn

    def forward_kv(c):
        for m in range(1, R // 2 + 1):
            d = 2 * m

            @pl.when(i - d >= 0)
            def _(d=d):
                kv_copy(d, c).wait_recv()

                @pl.when(core == 1)
                def _():
                    sib_copy(d, d - 1, c).start()

                if d + 1 <= R:
                    @pl.when(core == 0)
                    def _():
                        sib_copy(d, d + 1, c).start()

    def gather_step(c, carry):
        for k in range(1, T):
            @pl.when(t - k >= 0)
            def _(k=k):
                z_copy(t - k, c, 1, False).wait_recv()

                @pl.when(t + 1 < T)
                def _():
                    z_copy(t - k, c, 1, False).start()

            @pl.when(t + k < T)
            def _(k=k):
                z_copy(t + k, c, -1, False).wait_recv()

                @pl.when(t >= 1)
                def _():
                    z_copy(t + k, c, -1, False).start()

        @pl.when(c + 2 < C)
        def _():
            send_own(c + 2)

        r = rows_of(c)
        total = jnp.zeros((PAGE, 1), F32)
        for s in range(T):
            x = gath[s, r, :].astype(F32)
            total = total + jnp.sum(x * x, axis=1, keepdims=True)
        scale = lax.rsqrt(total / (T * width) + EPS)
        for s in range(T):
            cols = slice(s * width, (s + 1) * width)
            x = gath[s, r, :].astype(F32)
            nbuf[:, cols] = (x * scale * gain_ref[:, cols]).astype(BF16)
        n = nbuf[...]
        k_raw = jnp.dot(n, wk_ref[...], preferred_element_type=F32)
        v_raw = jnp.dot(n, wv_ref[...], preferred_element_type=F32)
        cs = cos_ref[r, :]
        sn = sin_ref[r, :]
        ok = valid_ref[r, :]
        for pair in range(HL // 2):
            cols = slice(pair * 128, (pair + 1) * 128)
            kr = rotated(k_raw[:, cols], cs, sn) * ok
            vr = v_raw[:, cols] * ok
            kv[0, r, pair * 256:pair * 256 + 128] = jnp.where(low, kr, pltpu.roll(vr, HD, 1)).astype(BF16)
            kv[0, r, pair * 256 + 128:pair * 256 + 256] = jnp.where(low, pltpu.roll(kr, HD, 1), vr).astype(BF16)
        for m in range(1, R // 2 + 1):
            @pl.when(i + 2 * m < S)
            def _(m=m):
                kv_copy(2 * m, c).start()

        @pl.when(core == 0)
        def _():
            sib_copy(0, 1, c).start()

        q_raw = jnp.dot(n, wq_ref[...], preferred_element_type=F32)
        for pair in range(HL // 2):
            cols = slice(pair * 128, (pair + 1) * 128)
            qr = rotated(q_raw[:, cols], cs, sn) * (HD ** -0.5)
            qpad[r, pair * 256:pair * 256 + 128] = jnp.where(low, qr, 0.0).astype(BF16)
            qpad[r, pair * 256 + 128:pair * 256 + 256] = jnp.where(low, pltpu.roll(qr, HD, 1), 0.0).astype(BF16)

        @pl.when(c == 0)
        def _():
            for k in range(1, T):
                wo_copy(lax.rem(t + k, T), t).wait_recv()
            for k in range(1, G):
                bc_copy(g, lax.rem(g + k, G)).start()

        @pl.when(c >= 1)
        def _():
            forward_kv(c - 1)
        return carry

    lax.fori_loop(0, C, gather_step, 0)
    forward_kv(C - 1)

    for d in range(1, R + 1):
        @pl.when(i >= d)
        def _(d=d):
            meta_copy(d).wait_recv()
            if d % 2 == 1:
                for c in range(C):
                    kv_copy(d, c).wait_recv()
    for k in range(1, G):
        bc_copy(lax.rem(g + k, G), g).wait_recv()

    keys = rows_all
    slot_count = cache_ref.shape[0]

    def attend_step(c, carry):
        @pl.when(c < C)
        def _():
            r = rows_of(c)
            seg = seg_ref[r, :][:, 0:1]
            q_place = c * PAGE + lax.broadcasted_iota(jnp.int32, (PAGE, keys), 0)
            k_place = lax.broadcasted_iota(jnp.int32, (PAGE, keys), 1)
            for d in range(R + 1):
                group = meta_ref[0:1, :] if d == 0 else meta[d - 1, 0:1, :]
                allowed = group == seg
                if d == 0:
                    allowed = allowed & (k_place <= q_place)
                bias[d] = jnp.where(allowed, 0.0, -1e30)
            outs = []
            for h in range(HL):
                cols = slice(h * 128, (h + 1) * 128)
                q = qpad[r, cols]
                scores = []
                top = None
                for d in range(R + 1):
                    s = lax.dot_general(q, kv[d, :, cols], (((1,), (1,)), ((), ())), preferred_element_type=F32) + bias[d]
                    scores.append(s)
                    here = jnp.max(s, axis=1, keepdims=True)
                    top = here if top is None else jnp.maximum(top, here)
                den = None
                acc = None
                for d in range(R + 1):
                    e = jnp.exp(scores[d] - top)
                    part = jnp.sum(e, axis=1, keepdims=True)
                    den = part if den is None else den + part
                    o = jnp.dot(e.astype(BF16), kv[d, :, cols], preferred_element_type=F32)
                    acc = o if acc is None else acc + o
                outs.append(acc / den)
            for pair in range(HL // 2):
                both = jnp.where(low, pltpu.roll(outs[2 * pair], HD, 1), outs[2 * pair + 1])
                att[t, r, pair * 128:(pair + 1) * 128] = both.astype(BF16)
            for k in range(1, T):
                att_copy(t, lax.rem(t + k, T), c).start()
            for j in range(slot_count // C):
                slot = c * (slot_count // C) + j
                page = jnp.zeros((PAGE, kv.shape[2]), BF16)
                for b in range(2):
                    for p in range(C):
                        src = meta_ref[8 + p:9 + p, :] if b == 0 else meta[0, 8 + p:9 + p, :]
                        hit = jnp.where(src == i * slot_count + slot, 1.0, 0.0).astype(BF16)
                        page = page + kv[b, p * PAGE:(p + 1) * PAGE, :] * hit
                cache_ref[slot] = page

        @pl.when(c >= 1)
        def _():
            r = rows_of(c - 1)
            for k in range(1, T):
                att_copy(lax.rem(t + k, T), t, c - 1).wait_recv()
            acc = res_ref[r, :].astype(F32)
            proj = jnp.dot(att[0, r, :], wo_all[0], preferred_element_type=F32)
            for s in range(1, T):
                proj = proj + jnp.dot(att[s, r, :], wo_all[s], preferred_element_type=F32)
            hid_ref[r, :] = (acc + proj).astype(BF16)
        return carry

    lax.fori_loop(0, C + 1, attend_step, 0)

    for k in range(1, T):
        wo_copy(t, lax.rem(t + k, T)).wait_send()
    for k in range(1, G):
        bc_copy(g, lax.rem(g + k, G)).wait_send()
    for d in range(1, R + 1):
        @pl.when(i + d < S)
        def _(d=d):
            meta_copy(d).wait_send()

    def drain(c, carry):
        for s in range(T):
            @pl.when((t + 1 < T) & (s <= t))
            def _(s=s):
                z_copy(s, c, 1, False).wait_send()

            @pl.when((t >= 1) & (s >= t))
            def _(s=s):
                z_copy(s, c, -1, False).wait_send()
        for m in range(1, R // 2 + 1):
            d = 2 * m

            @pl.when(i + d < S)
            def _(d=d):
                kv_copy(d, c).wait_send()

            @pl.when((i - d >= 0) & (core == 1))
            def _(d=d):
                sib_copy(d, d - 1, c).wait_send()

            if d + 1 <= R:
                @pl.when((i - d >= 0) & (core == 0))
                def _(d=d):
                    sib_copy(d, d + 1, c).wait_send()

        @pl.when(core == 0)
        def _():
            sib_copy(0, 1, c).wait_send()
        for k in range(1, T):
            att_copy(t, lax.rem(t + k, T), c).wait_send()
        return carry

    lax.fori_loop(0, C, drain, 0)


def body(
    S, T,
    residual, norm_gain, query_weight, key_weight, value_weight, out_weight, segment_start, token_valid, page_slot,
):
    rows, width = residual.shape
    local_heads = query_weight.shape[1] // HD
    R = min(SPAN, S // 2)
    G = min(8, S)
    C = rows // PAGE
    pages = page_slot.shape[0]
    slot_count = 2 * pages
    kvw = local_heads * 2 * HD
    first_row = lax.axis_index("seq") * rows
    offset = (first_row + jnp.arange(rows, dtype=jnp.int32) - segment_start).astype(F32)
    frequency = THETA ** (-2.0 * jnp.arange(HD // 2, dtype=F32) / HD)
    angles = offset[:, None] * frequency[None, :]
    cosine = jnp.cos(angles)
    sine = jnp.sin(angles)
    cos_t = jnp.concatenate([cosine] * 4, axis=1)
    sin_t = jnp.concatenate([-sine, sine, -sine, sine], axis=1)
    seg_t = jnp.broadcast_to(segment_start[:, None], (rows, 128))
    valid_t = jnp.broadcast_to((token_valid > 0).astype(F32)[:, None], (rows, 128))
    group = jnp.where(token_valid > 0, segment_start, -1)
    meta_t = jnp.concatenate([
        jnp.broadcast_to(group[None, :], (8, rows)),
        jnp.broadcast_to(page_slot[:, None], (pages, rows)),
        jnp.full((8 - pages, rows), -1, jnp.int32),
    ], axis=0)
    dma = pltpu.SemaphoreType.DMA
    vmem = pl.BlockSpec(memory_space=pltpu.VMEM)
    hidden, cache = pl.pallas_call(
        functools.partial(kernel, S, T, R, G),
        out_shape=(
            jax.ShapeDtypeStruct((rows, width), BF16),
            jax.ShapeDtypeStruct((slot_count, PAGE, kvw), BF16),
        ),
        in_specs=[vmem] * 11,
        out_specs=(vmem, vmem),
        scratch_shapes=[
            pltpu.VMEM((T, rows, width), BF16),
            pltpu.VMEM((PAGE, T * width), BF16),
            pltpu.VMEM((rows, kvw), BF16),
            pltpu.VMEM((R + 1, rows, kvw), BF16),
            pltpu.VMEM((R, 16, rows), jnp.int32),
            pltpu.VMEM((T, rows, local_heads * HD), BF16),
            pltpu.VMEM((T, local_heads * HD, width), BF16),
            pltpu.VMEM((R + 1, PAGE, rows), F32),
            dma((T, C)), dma((T, C)), dma((T, C)),
            dma((T,)), dma((T,)), dma((G,)), dma((G,)), dma((R,)), dma((R,)),
            dma((R + 1, C)), dma((R + 1, C)), dma((R + 1, C)), dma((T, C)), dma((T, C)),
        ],
        compiler_params=pltpu.CompilerParams(
            collective_id=0, has_side_effects=True, vmem_limit_bytes=56 * 1024 * 1024
        ),
        cost_estimate=pl.CostEstimate(flops=4 * 10**9, bytes_accessed=8 * 10**6, transcendentals=5 * 10**6),
    )(residual, norm_gain[None, :], query_weight, key_weight, value_weight, out_weight,
      cos_t, sin_t, seg_t, valid_t, meta_t)
    return hidden, cache


def solution(mesh):
    return jax.shard_map(
        functools.partial(body, mesh.shape["seq"], mesh.shape["tp"]),
        mesh=mesh,
        in_specs=(
            P("seq", "tp"),
            P(),
            P(None, "tp"),
            P(None, "tp"),
            P(None, "tp"),
            P("tp", None),
            P("seq"),
            P("seq"),
            P("seq"),
        ),
        out_specs=(P("seq", "tp"), P("seq", None, "tp")),
        check_vma=False,
    )
```

```python
import functools

import jax
import jax.numpy as jnp
from jax import lax
from jax.experimental import pallas as pl
from jax.experimental.pallas import tpu as pltpu
from jax.sharding import PartitionSpec as P

HD = 64
PAGE = 128
SPAN = 16
THETA = 130000.0
EPS = 1e-05
MESH = pl.DeviceIdType.MESH
F32 = jnp.float32
BF16 = jnp.bfloat16


def kernel(
    S, T, R, G,
    res_ref, gain_ref, freq_ref, wq_hbm, wk_hbm, wv_hbm, wo_ref, meta_ref,
    hid_ref, cache_ref,
    gath, nbuf, qpad, kv, meta, att, wo_all, seg_s, top_s, den_s, acc_s, wq_ref, wk_ref, wv_ref, w_sem,
    z_recv, zl_send, zr_send, wo_send, wo_recv, bc_send, bc_recv, meta_send, meta_recv,
    kv_send, kv_recv, sib_send, att_send, att_recv,
):
    i = lax.axis_index("seq")
    t = lax.axis_index("tp")
    rows_all, width = res_ref.shape
    C = rows_all // PAGE
    HL = wq_ref.shape[1] // HD
    core = lax.rem(i, 2)
    sib = i + 1 - 2 * core
    g = lax.rem(i, G)
    base = i - g
    wrows = wo_ref.shape[0] // G

    loads = [
        pltpu.make_async_copy(a, b, w_sem.at[n])
        for n, (a, b) in enumerate(((wk_hbm, wk_ref), (wv_hbm, wv_ref), (wq_hbm, wq_ref)))
    ]
    for load in loads:
        load.start()

    far = max(R, G - 1)
    barrier = pltpu.get_barrier_semaphore()
    for d in range(1, far + 1):
        @pl.when(i + d < S)
        def _(d=d):
            pl.semaphore_signal(barrier, inc=1, device_id=(i + d, t), device_id_type=MESH)

        @pl.when(i - d >= 0)
        def _(d=d):
            pl.semaphore_signal(barrier, inc=1, device_id=(i - d, t), device_id_type=MESH)
    for k in range(1, T):
        pl.semaphore_signal(barrier, inc=1, device_id=(i, lax.rem(t + k, T)), device_id_type=MESH)
    pl.semaphore_wait(barrier, jnp.minimum(i, far) + jnp.minimum(S - 1 - i, far) + (T - 1))

    def rows_of(c):
        return pl.ds(pl.multiple_of(c * PAGE, PAGE), PAGE)

    Q = rows_all // 2

    def half_of(a):
        return pl.ds(pl.multiple_of(a * Q, Q), Q)

    def wo_copy(s, to):
        r = pl.ds(pl.multiple_of(g * wrows, wrows), wrows)
        return pltpu.make_async_remote_copy(
            src_ref=wo_ref.at[r, pl.ds(pl.multiple_of(to * width, width), width)],
            dst_ref=wo_all.at[s, r, :],
            send_sem=wo_send.at[to], recv_sem=wo_recv.at[s],
            device_id=(i, to), device_id_type=MESH)

    def bc_copy(owner, to):
        r = pl.ds(pl.multiple_of(owner * wrows, wrows), wrows)
        return pltpu.make_async_remote_copy(
            src_ref=wo_all.at[:, r, :], dst_ref=wo_all.at[:, r, :],
            send_sem=bc_send.at[to], recv_sem=bc_recv.at[owner],
            device_id=(base + to, t), device_id_type=MESH)

    def meta_copy(d):
        return pltpu.make_async_remote_copy(
            src_ref=meta_ref, dst_ref=meta.at[d - 1],
            send_sem=meta_send.at[d - 1], recv_sem=meta_recv.at[d - 1],
            device_id=(i + d, t), device_id_type=MESH)

    def z_copy(s, c, step, own):
        r = rows_of(c)
        sems = zr_send if step > 0 else zl_send
        return pltpu.make_async_remote_copy(
            src_ref=res_ref.at[r, :] if own else gath.at[s, r, :],
            dst_ref=gath.at[s, r, :],
            send_sem=sems.at[s, c], recv_sem=z_recv.at[s, c],
            device_id=(i, t + step), device_id_type=MESH)

    def kv_copy(d, c):
        r = rows_of(c)
        return pltpu.make_async_remote_copy(
            src_ref=kv.at[0, r, :], dst_ref=kv.at[d, r, :],
            send_sem=kv_send.at[d, c], recv_sem=kv_recv.at[d, c],
            device_id=(i + d, t), device_id_type=MESH)

    def sib_copy(src, dst, c):
        r = rows_of(c)
        return pltpu.make_async_remote_copy(
            src_ref=kv.at[src, r, :], dst_ref=kv.at[dst, r, :],
            send_sem=sib_send.at[dst, c], recv_sem=kv_recv.at[dst, c],
            device_id=(sib, t), device_id_type=MESH)

    def att_copy(s, to, c):
        r = half_of(c)
        return pltpu.make_async_remote_copy(
            src_ref=att.at[s, r, :], dst_ref=att.at[s, r, :],
            send_sem=att_send.at[to, c], recv_sem=att_recv.at[s, c],
            device_id=(i, to), device_id_type=MESH)

    def send_own(c):
        @pl.when(t + 1 < T)
        def _():
            z_copy(t, c, 1, True).start()

        @pl.when(t >= 1)
        def _():
            z_copy(t, c, -1, True).start()

    send_own(0)
    for k in range(1, T):
        wo_copy(t, lax.rem(t + k, T)).start()
    if C > 1:
        send_own(1)
    for d in range(1, R + 1):
        @pl.when(i + d < S)
        def _(d=d):
            meta_copy(d).start()

    gath[t] = res_ref[...]
    top_s[...] = jnp.full(top_s.shape, -1e30, F32)
    den_s[...] = jnp.zeros(den_s.shape, F32)
    acc_s[...] = jnp.zeros(acc_s.shape, F32)
    mine = pl.ds(pl.multiple_of(g * wrows, wrows), wrows)
    wo_all[t, mine, :] = wo_ref[mine, pl.ds(pl.multiple_of(t * width, width), width)]
    for d in range(1, R + 1):
        @pl.when(i < d)
        def _(d=d):
            kv[d] = jnp.zeros(kv.shape[1:], BF16)
            meta[d - 1] = jnp.full(meta.shape[1:], -1, jnp.int32)

    lane128 = lax.broadcasted_iota(jnp.int32, (PAGE, 128), 1)
    low = lane128 < HD
    first = lax.rem(lane128, HD) < HD // 2

    def rotated(x, cs, sn):
        fwd = pltpu.roll(x, 128 - HD // 2, 1)
        back = pltpu.roll(x, HD // 2, 1)
        return x * cs + jnp.where(first, fwd, back) * sn

    def forward_kv(c):
        for m in range(1, R // 2 + 1):
            d = 2 * m

            @pl.when(i - d >= 0)
            def _(d=d):
                kv_copy(d, c).wait_recv()

                @pl.when(core == 1)
                def _():
                    sib_copy(d, d - 1, c).start()

                if d + 1 <= R:
                    @pl.when(core == 0)
                    def _():
                        sib_copy(d, d + 1, c).start()

    def wait_odd(c):
        for d in range(1, R + 1, 2):
            @pl.when(i >= d)
            def _(d=d):
                kv_copy(d, c).wait_recv()

    def attend(a, c):
        qr, kr = half_of(a), rows_of(c)
        seg = seg_s[qr, :]
        q_place = a * Q + lax.broadcasted_iota(jnp.int32, (Q, PAGE), 0)
        k_place = c * PAGE + lax.broadcasted_iota(jnp.int32, (Q, PAGE), 1)
        masks = []
        for d in range(R + 1):
            group = meta_ref[0:1, kr] if d == 0 else meta[d - 1, 0:1, kr]
            allowed = group == seg
            if d == 0:
                allowed = allowed & (k_place <= q_place)
            masks.append(jnp.where(allowed, 0.0, -1e30))
        for h in range(HL):
            cols = slice(h * 128, (h + 1) * 128)
            q = qpad[qr, cols]
            scores = []
            most = None
            for d in range(R + 1):
                s = lax.dot_general(q, kv[d, kr, cols], (((1,), (1,)), ((), ())), preferred_element_type=F32) + masks[d]
                scores.append(s)
                most = s if most is None else jnp.maximum(most, s)
            old = top_s[a, h]
            top = jnp.maximum(old, jnp.max(most, axis=1, keepdims=True))
            part = None
            acc = None
            for d in range(R + 1):
                e = jnp.exp(scores[d] - top)
                part = e if part is None else part + e
                o = jnp.dot(e.astype(BF16), kv[d, kr, cols], preferred_element_type=F32)
                acc = o if acc is None else acc + o
            shrink = jnp.exp(old - top)
            top_s[a, h] = top
            den_s[a, h] = den_s[a, h] * shrink + jnp.sum(part, axis=1, keepdims=True)
            acc_s[a, h] = acc_s[a, h] * shrink + acc

    def gather_step(c, carry):
        r = rows_of(c)

        def column(row):
            return jnp.transpose(jnp.broadcast_to(row.astype(F32), (PAGE, 128)))

        seg_col = column(meta_ref[12:13, r])
        ok = column(meta_ref[13:14, r])
        seg_s[r, :] = seg_col.astype(jnp.int32)
        place = (i * rows_all + c * PAGE + lax.broadcasted_iota(jnp.int32, (PAGE, 128), 0)).astype(F32)
        angles = (place - seg_col) * freq_ref[...]
        cs = jnp.cos(angles)
        sn = jnp.sin(angles)
        sn = jnp.where(first, -sn, sn)
        for k in range(1, T):
            @pl.when(t - k >= 0)
            def _(k=k):
                z_copy(t - k, c, 1, False).wait_recv()

                @pl.when(t + 1 < T)
                def _():
                    z_copy(t - k, c, 1, False).start()

            @pl.when(t + k < T)
            def _(k=k):
                z_copy(t + k, c, -1, False).wait_recv()

                @pl.when(t >= 1)
                def _():
                    z_copy(t + k, c, -1, False).start()

        @pl.when(c + 2 < C)
        def _():
            send_own(c + 2)

        @pl.when(c == 0)
        def _():
            for load in loads:
                load.wait()

        total = jnp.zeros((PAGE, 1), F32)
        for s in range(T):
            x = gath[s, r, :].astype(F32)
            total = total + jnp.sum(x * x, axis=1, keepdims=True)
        scale = lax.rsqrt(total / (T * width) + EPS)
        for s in range(T):
            cols = slice(s * width, (s + 1) * width)
            x = gath[s, r, :].astype(F32)
            nbuf[:, cols] = (x * scale * gain_ref[:, cols]).astype(BF16)
        n = nbuf[...]
        k_raw = jnp.dot(n, wk_ref[...], preferred_element_type=F32)
        v_raw = jnp.dot(n, wv_ref[...], preferred_element_type=F32)
        for pair in range(HL // 2):
            cols = slice(pair * 128, (pair + 1) * 128)
            kr = rotated(k_raw[:, cols], cs, sn) * ok
            vr = v_raw[:, cols] * ok
            kv[0, r, pair * 256:pair * 256 + 128] = jnp.where(low, kr, pltpu.roll(vr, HD, 1)).astype(BF16)
            kv[0, r, pair * 256 + 128:pair * 256 + 256] = jnp.where(low, pltpu.roll(kr, HD, 1), vr).astype(BF16)
        for m in range(1, R // 2 + 1):
            @pl.when(i + 2 * m < S)
            def _(m=m):
                kv_copy(2 * m, c).start()

        @pl.when(core == 0)
        def _():
            sib_copy(0, 1, c).start()

        q_raw = jnp.dot(n, wq_ref[...], preferred_element_type=F32)
        for pair in range(HL // 2):
            cols = slice(pair * 128, (pair + 1) * 128)
            qr = rotated(q_raw[:, cols], cs, sn) * (HD ** -0.5)
            qpad[r, pair * 256:pair * 256 + 128] = jnp.where(low, qr, 0.0).astype(BF16)
            qpad[r, pair * 256 + 128:pair * 256 + 256] = jnp.where(low, pltpu.roll(qr, HD, 1), 0.0).astype(BF16)

        @pl.when(c == 0)
        def _():
            for k in range(1, T):
                wo_copy(lax.rem(t + k, T), t).wait_recv()
            for k in range(1, G):
                bc_copy(g, lax.rem(g + k, G)).start()

        @pl.when(c >= 1)
        def _():
            forward_kv(c - 1)

        @pl.when(c == 2)
        def _():
            for d in range(1, R + 1):
                @pl.when(i >= d)
                def _(d=d):
                    meta_copy(d).wait_recv()

        @pl.when(c >= 2)
        def _():
            wait_odd(c - 2)
            attend(0, c - 2)
        return carry

    lax.fori_loop(0, C, gather_step, 0)

    def attend_step(n, carry):
        a = jnp.where(n < 2, 1, lax.rem(n, 2))
        c = jnp.where(n < 2, n, n // 2 + 1)

        @pl.when(n == 1)
        def _():
            forward_kv(C - 1)

        @pl.when((n == 2) | (n == 4))
        def _():
            wait_odd(c)

        attend(a, c)

        @pl.when(n >= 4)
        def _():
            r = half_of(a)
            low_q = lax.broadcasted_iota(jnp.int32, (Q, 128), 1) < HD
            for pair in range(HL // 2):
                one = acc_s[a, 2 * pair] / den_s[a, 2 * pair]
                two = acc_s[a, 2 * pair + 1] / den_s[a, 2 * pair + 1]
                both = jnp.where(low_q, pltpu.roll(one, HD, 1), two)
                att[t, r, pair * 128:(pair + 1) * 128] = both.astype(BF16)
            for k in range(1, T):
                att_copy(t, lax.rem(t + k, T), a).start()
        return carry

    lax.fori_loop(0, 6, attend_step, 0)

    slot_count = cache_ref.shape[0]

    def cache_step(slot, carry):
        page = jnp.zeros((PAGE, kv.shape[2]), BF16)
        for b in range(2):
            for p in range(C):
                src = meta_ref[8 + p:9 + p, :] if b == 0 else meta[0, 8 + p:9 + p, :]
                hit = jnp.where(src == i * slot_count + slot, 1.0, 0.0).astype(BF16)
                page = page + kv[b, p * PAGE:(p + 1) * PAGE, :] * hit
        cache_ref[slot] = page
        return carry

    lax.fori_loop(0, slot_count, cache_step, 0)

    for k in range(1, G):
        bc_copy(lax.rem(g + k, G), g).wait_recv()

    def project_step(a, carry):
        r = half_of(a)
        for k in range(1, T):
            att_copy(lax.rem(t + k, T), t, a).wait_recv()
        proj = jnp.dot(att[0, r, :], wo_all[0], preferred_element_type=F32)
        for s in range(1, T):
            proj = proj + jnp.dot(att[s, r, :], wo_all[s], preferred_element_type=F32)
        hid_ref[r, :] = (res_ref[r, :].astype(F32) + proj).astype(BF16)
        return carry

    lax.fori_loop(0, 2, project_step, 0)

    for k in range(1, T):
        wo_copy(t, lax.rem(t + k, T)).wait_send()
    for k in range(1, G):
        bc_copy(g, lax.rem(g + k, G)).wait_send()
    for d in range(1, R + 1):
        @pl.when(i + d < S)
        def _(d=d):
            meta_copy(d).wait_send()

    def drain(c, carry):
        for s in range(T):
            @pl.when((t + 1 < T) & (s <= t))
            def _(s=s):
                z_copy(s, c, 1, False).wait_send()

            @pl.when((t >= 1) & (s >= t))
            def _(s=s):
                z_copy(s, c, -1, False).wait_send()
        for m in range(1, R // 2 + 1):
            d = 2 * m

            @pl.when(i + d < S)
            def _(d=d):
                kv_copy(d, c).wait_send()

            @pl.when((i - d >= 0) & (core == 1))
            def _(d=d):
                sib_copy(d, d - 1, c).wait_send()

            if d + 1 <= R:
                @pl.when((i - d >= 0) & (core == 0))
                def _(d=d):
                    sib_copy(d, d + 1, c).wait_send()

        @pl.when(core == 0)
        def _():
            sib_copy(0, 1, c).wait_send()
        return carry

    lax.fori_loop(0, C, drain, 0)
    for a in range(2):
        for k in range(1, T):
            att_copy(t, lax.rem(t + k, T), a).wait_send()


def body(
    S, T,
    residual, norm_gain, query_weight, key_weight, value_weight, out_weight, segment_start, token_valid, page_slot,
):
    rows, width = residual.shape
    local_heads = query_weight.shape[1] // HD
    R = min(SPAN, S // 2)
    G = min(8, S)
    C = rows // PAGE
    pages = page_slot.shape[0]
    slot_count = 2 * pages
    kvw = local_heads * 2 * HD
    frequency = THETA ** (-2.0 * jnp.arange(HD // 2, dtype=F32) / HD)
    freq_t = jnp.concatenate([frequency] * 4)[None, :]
    group = jnp.where(token_valid > 0, segment_start, -1)
    meta_t = jnp.concatenate([
        jnp.broadcast_to(group[None, :], (8, rows)),
        jnp.broadcast_to(page_slot[:, None], (pages, rows)),
        segment_start[None, :],
        (token_valid > 0).astype(jnp.int32)[None, :],
        jnp.full((6 - pages, rows), -1, jnp.int32),
    ], axis=0)
    dma = pltpu.SemaphoreType.DMA
    vmem = pl.BlockSpec(memory_space=pltpu.VMEM)
    hidden, cache = pl.pallas_call(
        functools.partial(kernel, S, T, R, G),
        out_shape=(
            jax.ShapeDtypeStruct((rows, width), BF16),
            jax.ShapeDtypeStruct((slot_count, PAGE, kvw), BF16),
        ),
        in_specs=[vmem] * 3 + [pl.BlockSpec(memory_space=pl.ANY)] * 3 + [vmem] * 2,
        out_specs=(vmem, vmem),
        scratch_shapes=[
            pltpu.VMEM((T, rows, width), BF16),
            pltpu.VMEM((PAGE, T * width), BF16),
            pltpu.VMEM((rows, kvw), BF16),
            pltpu.VMEM((R + 1, rows, kvw), BF16),
            pltpu.VMEM((R, 16, rows), jnp.int32),
            pltpu.VMEM((T, rows, local_heads * HD), BF16),
            pltpu.VMEM((T, local_heads * HD, width), BF16),
            pltpu.VMEM((rows, 128), jnp.int32),
            pltpu.VMEM((2, local_heads, rows // 2, 1), F32),
            pltpu.VMEM((2, local_heads, rows // 2, 1), F32),
            pltpu.VMEM((2, local_heads, rows // 2, 128), F32),
            pltpu.VMEM(query_weight.shape, BF16),
            pltpu.VMEM(query_weight.shape, BF16),
            pltpu.VMEM(query_weight.shape, BF16),
            dma((3,)),
            dma((T, C)), dma((T, C)), dma((T, C)),
            dma((T,)), dma((T,)), dma((G,)), dma((G,)), dma((R,)), dma((R,)),
            dma((R + 1, C)), dma((R + 1, C)), dma((R + 1, C)), dma((T, 2)), dma((T, 2)),
        ],
        compiler_params=pltpu.CompilerParams(
            collective_id=0, has_side_effects=True, vmem_limit_bytes=56 * 1024 * 1024
        ),
        cost_estimate=pl.CostEstimate(flops=4 * 10**9, bytes_accessed=8 * 10**6, transcendentals=5 * 10**6),
    )(residual, norm_gain[None, :], freq_t, query_weight, key_weight, value_weight, out_weight, meta_t)
    return hidden, cache


def solution(mesh):
    return jax.shard_map(
        functools.partial(body, mesh.shape["seq"], mesh.shape["tp"]),
        mesh=mesh,
        in_specs=(
            P("seq", "tp"),
            P(),
            P(None, "tp"),
            P(None, "tp"),
            P(None, "tp"),
            P("tp", None),
            P("seq"),
            P("seq"),
            P("seq"),
        ),
        out_specs=(P("seq", "tp"), P("seq", None, "tp")),
        check_vma=False,
    )
```

```python
import functools

import jax
import jax.numpy as jnp
from jax import lax
from jax.experimental import pallas as pl
from jax.experimental.pallas import tpu as pltpu
from jax.sharding import PartitionSpec as P

HD = 64
PAGE = 128
SPAN = 16
THETA = 130000.0
EPS = 1e-05
MESH = pl.DeviceIdType.MESH
F32 = jnp.float32
BF16 = jnp.bfloat16


def kernel(
    S, T, R, G,
    res_ref, gain_ref, freq_ref, wq_hbm, wk_hbm, wv_hbm, wo_ref, meta_ref,
    hid_ref, cache_ref,
    gath, nbuf, qpad, kv, meta, att, wo_all, seg_s, top_s, den_s, acc_s, wq_ref, wk_ref, wv_ref, w_sem,
    z_recv, zl_send, zr_send, wo_send, wo_recv, bc_send, bc_recv, meta_send, meta_recv,
    kv_send, kv_recv, sib_send, att_send, att_recv,
):
    i = lax.axis_index("seq")
    t = lax.axis_index("tp")
    rows_all, width = res_ref.shape
    C = rows_all // PAGE
    HL = wq_ref.shape[1] // HD
    core = lax.rem(i, 2)
    sib = i + 1 - 2 * core
    g = lax.rem(i, G)
    base = i - g
    wrows = wo_ref.shape[0] // G

    loads = [
        pltpu.make_async_copy(a, b, w_sem.at[n])
        for n, (a, b) in enumerate(((wk_hbm, wk_ref), (wv_hbm, wv_ref), (wq_hbm, wq_ref)))
    ]
    for load in loads:
        load.start()

    far = max(R, G - 1)
    barrier = pltpu.get_barrier_semaphore()
    for d in range(1, far + 1):
        @pl.when(i + d < S)
        def _(d=d):
            pl.semaphore_signal(barrier, inc=1, device_id=(i + d, t), device_id_type=MESH)

        @pl.when(i - d >= 0)
        def _(d=d):
            pl.semaphore_signal(barrier, inc=1, device_id=(i - d, t), device_id_type=MESH)
    for k in range(1, T):
        pl.semaphore_signal(barrier, inc=1, device_id=(i, lax.rem(t + k, T)), device_id_type=MESH)
    pl.semaphore_wait(barrier, jnp.minimum(i, far) + jnp.minimum(S - 1 - i, far) + (T - 1))

    def rows_of(c):
        return pl.ds(pl.multiple_of(c * PAGE, PAGE), PAGE)

    Q = rows_all // 2

    def half_of(a):
        return pl.ds(pl.multiple_of(a * Q, Q), Q)

    def wo_copy(s, to):
        r = pl.ds(pl.multiple_of(g * wrows, wrows), wrows)
        return pltpu.make_async_remote_copy(
            src_ref=wo_ref.at[r, pl.ds(pl.multiple_of(to * width, width), width)],
            dst_ref=wo_all.at[s, r, :],
            send_sem=wo_send.at[to], recv_sem=wo_recv.at[s],
            device_id=(i, to), device_id_type=MESH)

    def bc_copy(owner, to):
        r = pl.ds(pl.multiple_of(owner * wrows, wrows), wrows)
        return pltpu.make_async_remote_copy(
            src_ref=wo_all.at[:, r, :], dst_ref=wo_all.at[:, r, :],
            send_sem=bc_send.at[to], recv_sem=bc_recv.at[owner],
            device_id=(base + to, t), device_id_type=MESH)

    def meta_copy(d):
        return pltpu.make_async_remote_copy(
            src_ref=meta_ref, dst_ref=meta.at[d - 1],
            send_sem=meta_send.at[d - 1], recv_sem=meta_recv.at[d - 1],
            device_id=(i + d, t), device_id_type=MESH)

    def z_copy(s, c, step, own):
        r = rows_of(c)
        sems = zr_send if step > 0 else zl_send
        return pltpu.make_async_remote_copy(
            src_ref=res_ref.at[r, :] if own else gath.at[s, r, :],
            dst_ref=gath.at[s, r, :],
            send_sem=sems.at[s, c], recv_sem=z_recv.at[s, c],
            device_id=(i, t + step), device_id_type=MESH)

    def kv_copy(d, c):
        r = rows_of(c)
        return pltpu.make_async_remote_copy(
            src_ref=kv.at[0, r, :], dst_ref=kv.at[d, r, :],
            send_sem=kv_send.at[d, c], recv_sem=kv_recv.at[d, c],
            device_id=(i + d, t), device_id_type=MESH)

    def sib_copy(src, dst, c):
        r = rows_of(c)
        return pltpu.make_async_remote_copy(
            src_ref=kv.at[src, r, :], dst_ref=kv.at[dst, r, :],
            send_sem=sib_send.at[dst, c], recv_sem=kv_recv.at[dst, c],
            device_id=(sib, t), device_id_type=MESH)

    def att_copy(s, to, c):
        r = half_of(c)
        return pltpu.make_async_remote_copy(
            src_ref=att.at[s, r, :], dst_ref=att.at[s, r, :],
            send_sem=att_send.at[to, c], recv_sem=att_recv.at[s, c],
            device_id=(i, to), device_id_type=MESH)

    def send_own(c):
        @pl.when(t + 1 < T)
        def _():
            z_copy(t, c, 1, True).start()

        @pl.when(t >= 1)
        def _():
            z_copy(t, c, -1, True).start()

    send_own(0)
    if C > 1:
        send_own(1)
    for d in range(1, R + 1):
        @pl.when(i + d < S)
        def _(d=d):
            meta_copy(d).start()

    gath[t] = res_ref[...]
    top_s[...] = jnp.full(top_s.shape, -1e30, F32)
    den_s[...] = jnp.zeros(den_s.shape, F32)
    acc_s[...] = jnp.zeros(acc_s.shape, F32)
    mine = pl.ds(pl.multiple_of(g * wrows, wrows), wrows)
    wo_all[t, mine, :] = wo_ref[mine, pl.ds(pl.multiple_of(t * width, width), width)]
    for d in range(1, R + 1):
        @pl.when(i < d)
        def _(d=d):
            kv[d] = jnp.zeros(kv.shape[1:], BF16)
            meta[d - 1] = jnp.full(meta.shape[1:], -1, jnp.int32)

    lane128 = lax.broadcasted_iota(jnp.int32, (PAGE, 128), 1)
    low = lane128 < HD
    first = lax.rem(lane128, HD) < HD // 2

    def rotated(x, cs, sn):
        fwd = pltpu.roll(x, 128 - HD // 2, 1)
        back = pltpu.roll(x, HD // 2, 1)
        return x * cs + jnp.where(first, fwd, back) * sn

    def forward_kv(c):
        for m in range(1, R // 2 + 1):
            d = 2 * m

            @pl.when(i - d >= 0)
            def _(d=d):
                kv_copy(d, c).wait_recv()

                @pl.when(core == 1)
                def _():
                    sib_copy(d, d - 1, c).start()

                if d + 1 <= R:
                    @pl.when(core == 0)
                    def _():
                        sib_copy(d, d + 1, c).start()

    def wait_odd(c):
        for d in range(1, R + 1, 2):
            @pl.when(i >= d)
            def _(d=d):
                kv_copy(d, c).wait_recv()

    def attend(a, c):
        qr, kr = half_of(a), rows_of(c)
        seg = seg_s[qr, :]
        q_place = a * Q + lax.broadcasted_iota(jnp.int32, (Q, PAGE), 0)
        k_place = c * PAGE + lax.broadcasted_iota(jnp.int32, (Q, PAGE), 1)
        masks = []
        for d in range(R + 1):
            group = meta_ref[0:1, kr] if d == 0 else meta[d - 1, 0:1, kr]
            allowed = group == seg
            if d == 0:
                allowed = allowed & (k_place <= q_place)
            masks.append(jnp.where(allowed, 0.0, -1e30))
        for h in range(HL):
            cols = slice(h * 128, (h + 1) * 128)
            q = qpad[qr, cols]
            scores = []
            most = None
            for d in range(R + 1):
                s = lax.dot_general(q, kv[d, kr, cols], (((1,), (1,)), ((), ())), preferred_element_type=F32) + masks[d]
                scores.append(s)
                most = s if most is None else jnp.maximum(most, s)
            old = top_s[a, h]
            top = jnp.maximum(old, jnp.max(most, axis=1, keepdims=True))
            part = None
            acc = None
            for d in range(R + 1):
                e = jnp.exp(scores[d] - top)
                part = e if part is None else part + e
                o = jnp.dot(e.astype(BF16), kv[d, kr, cols], preferred_element_type=F32)
                acc = o if acc is None else acc + o
            shrink = jnp.exp(old - top)
            top_s[a, h] = top
            den_s[a, h] = den_s[a, h] * shrink + jnp.sum(part, axis=1, keepdims=True)
            acc_s[a, h] = acc_s[a, h] * shrink + acc

    def gather_step(c, carry):
        r = rows_of(c)

        def column(row):
            return jnp.transpose(jnp.broadcast_to(row.astype(F32), (PAGE, 128)))

        seg_col = column(meta_ref[12:13, r])
        ok = column(meta_ref[13:14, r])
        seg_s[r, :] = seg_col.astype(jnp.int32)
        place = (i * rows_all + c * PAGE + lax.broadcasted_iota(jnp.int32, (PAGE, 128), 0)).astype(F32)
        angles = (place - seg_col) * freq_ref[...]
        cs = jnp.cos(angles)
        sn = jnp.sin(angles)
        sn = jnp.where(first, -sn, sn)
        for k in range(1, T):
            @pl.when(t - k >= 0)
            def _(k=k):
                z_copy(t - k, c, 1, False).wait_recv()

                @pl.when(t + 1 < T)
                def _():
                    z_copy(t - k, c, 1, False).start()

            @pl.when(t + k < T)
            def _(k=k):
                z_copy(t + k, c, -1, False).wait_recv()

                @pl.when(t >= 1)
                def _():
                    z_copy(t + k, c, -1, False).start()

        @pl.when(c + 2 < C)
        def _():
            send_own(c + 2)

        @pl.when(c == 0)
        def _():
            for load in loads:
                load.wait()

        total = jnp.zeros((PAGE, 1), F32)
        for s in range(T):
            x = gath[s, r, :].astype(F32)
            total = total + jnp.sum(x * x, axis=1, keepdims=True)
        scale = lax.rsqrt(total / (T * width) + EPS)
        for s in range(T):
            cols = slice(s * width, (s + 1) * width)
            x = gath[s, r, :].astype(F32)
            nbuf[:, cols] = (x * scale * gain_ref[:, cols]).astype(BF16)
        n = nbuf[...]
        k_raw = jnp.dot(n, wk_ref[...], preferred_element_type=F32)
        v_raw = jnp.dot(n, wv_ref[...], preferred_element_type=F32)
        for pair in range(HL // 2):
            cols = slice(pair * 128, (pair + 1) * 128)
            kr = rotated(k_raw[:, cols], cs, sn) * ok
            vr = v_raw[:, cols] * ok
            kv[0, r, pair * 256:pair * 256 + 128] = jnp.where(low, kr, pltpu.roll(vr, HD, 1)).astype(BF16)
            kv[0, r, pair * 256 + 128:pair * 256 + 256] = jnp.where(low, pltpu.roll(kr, HD, 1), vr).astype(BF16)
        for m in range(1, R // 2 + 1):
            @pl.when(i + 2 * m < S)
            def _(m=m):
                kv_copy(2 * m, c).start()

        @pl.when(core == 0)
        def _():
            sib_copy(0, 1, c).start()

        q_raw = jnp.dot(n, wq_ref[...], preferred_element_type=F32)
        for pair in range(HL // 2):
            cols = slice(pair * 128, (pair + 1) * 128)
            qr = rotated(q_raw[:, cols], cs, sn) * (HD ** -0.5)
            qpad[r, pair * 256:pair * 256 + 128] = jnp.where(low, qr, 0.0).astype(BF16)
            qpad[r, pair * 256 + 128:pair * 256 + 256] = jnp.where(low, pltpu.roll(qr, HD, 1), 0.0).astype(BF16)

        @pl.when(c >= 1)
        def _():
            forward_kv(c - 1)

        @pl.when(c == 2)
        def _():
            for d in range(1, R + 1):
                @pl.when(i >= d)
                def _(d=d):
                    meta_copy(d).wait_recv()

        @pl.when(c >= 2)
        def _():
            wait_odd(c - 2)
            attend(0, c - 2)
        return carry

    lax.fori_loop(0, C, gather_step, 0)

    for k in range(1, T):
        wo_copy(t, lax.rem(t + k, T)).start()

    def attend_step(n, carry):
        a = jnp.where(n < 2, 1, lax.rem(n, 2))
        c = jnp.where(n < 2, n, n // 2 + 1)

        @pl.when(n == 1)
        def _():
            forward_kv(C - 1)

        @pl.when((n == 2) | (n == 4))
        def _():
            wait_odd(c)

        @pl.when(n == 4)
        def _():
            for k in range(1, T):
                wo_copy(lax.rem(t + k, T), t).wait_recv()
            for k in range(1, G):
                bc_copy(g, lax.rem(g + k, G)).start()

        attend(a, c)

        @pl.when(n >= 4)
        def _():
            r = half_of(a)
            low_q = lax.broadcasted_iota(jnp.int32, (Q, 128), 1) < HD
            for pair in range(HL // 2):
                one = acc_s[a, 2 * pair] / den_s[a, 2 * pair]
                two = acc_s[a, 2 * pair + 1] / den_s[a, 2 * pair + 1]
                both = jnp.where(low_q, pltpu.roll(one, HD, 1), two)
                att[t, r, pair * 128:(pair + 1) * 128] = both.astype(BF16)
            for k in range(1, T):
                att_copy(t, lax.rem(t + k, T), a).start()
        return carry

    lax.fori_loop(0, 6, attend_step, 0)

    slot_count = cache_ref.shape[0]

    def cache_step(slot, carry):
        page = jnp.zeros((PAGE, kv.shape[2]), BF16)
        for b in range(2):
            for p in range(C):
                src = meta_ref[8 + p:9 + p, :] if b == 0 else meta[0, 8 + p:9 + p, :]
                hit = jnp.where(src == i * slot_count + slot, 1.0, 0.0).astype(BF16)
                page = page + kv[b, p * PAGE:(p + 1) * PAGE, :] * hit
        cache_ref[slot] = page
        return carry

    lax.fori_loop(0, slot_count, cache_step, 0)

    for k in range(1, G):
        bc_copy(lax.rem(g + k, G), g).wait_recv()

    def project_step(a, carry):
        r = half_of(a)
        for k in range(1, T):
            att_copy(lax.rem(t + k, T), t, a).wait_recv()
        proj = jnp.dot(att[0, r, :], wo_all[0], preferred_element_type=F32)
        for s in range(1, T):
            proj = proj + jnp.dot(att[s, r, :], wo_all[s], preferred_element_type=F32)
        hid_ref[r, :] = (res_ref[r, :].astype(F32) + proj).astype(BF16)
        return carry

    lax.fori_loop(0, 2, project_step, 0)

    for k in range(1, T):
        wo_copy(t, lax.rem(t + k, T)).wait_send()
    for k in range(1, G):
        bc_copy(g, lax.rem(g + k, G)).wait_send()
    for d in range(1, R + 1):
        @pl.when(i + d < S)
        def _(d=d):
            meta_copy(d).wait_send()

    def drain(c, carry):
        for s in range(T):
            @pl.when((t + 1 < T) & (s <= t))
            def _(s=s):
                z_copy(s, c, 1, False).wait_send()

            @pl.when((t >= 1) & (s >= t))
            def _(s=s):
                z_copy(s, c, -1, False).wait_send()
        for m in range(1, R // 2 + 1):
            d = 2 * m

            @pl.when(i + d < S)
            def _(d=d):
                kv_copy(d, c).wait_send()

            @pl.when((i - d >= 0) & (core == 1))
            def _(d=d):
                sib_copy(d, d - 1, c).wait_send()

            if d + 1 <= R:
                @pl.when((i - d >= 0) & (core == 0))
                def _(d=d):
                    sib_copy(d, d + 1, c).wait_send()

        @pl.when(core == 0)
        def _():
            sib_copy(0, 1, c).wait_send()
        return carry

    lax.fori_loop(0, C, drain, 0)
    for a in range(2):
        for k in range(1, T):
            att_copy(t, lax.rem(t + k, T), a).wait_send()


def body(
    S, T,
    residual, norm_gain, query_weight, key_weight, value_weight, out_weight, segment_start, token_valid, page_slot,
):
    rows, width = residual.shape
    local_heads = query_weight.shape[1] // HD
    R = min(SPAN, S // 2)
    G = min(8, S)
    C = rows // PAGE
    pages = page_slot.shape[0]
    slot_count = 2 * pages
    kvw = local_heads * 2 * HD
    frequency = THETA ** (-2.0 * jnp.arange(HD // 2, dtype=F32) / HD)
    freq_t = jnp.concatenate([frequency] * 4)[None, :]
    group = jnp.where(token_valid > 0, segment_start, -1)
    meta_t = jnp.concatenate([
        jnp.broadcast_to(group[None, :], (8, rows)),
        jnp.broadcast_to(page_slot[:, None], (pages, rows)),
        segment_start[None, :],
        (token_valid > 0).astype(jnp.int32)[None, :],
        jnp.full((6 - pages, rows), -1, jnp.int32),
    ], axis=0)
    dma = pltpu.SemaphoreType.DMA
    vmem = pl.BlockSpec(memory_space=pltpu.VMEM)
    hidden, cache = pl.pallas_call(
        functools.partial(kernel, S, T, R, G),
        out_shape=(
            jax.ShapeDtypeStruct((rows, width), BF16),
            jax.ShapeDtypeStruct((slot_count, PAGE, kvw), BF16),
        ),
        in_specs=[vmem] * 3 + [pl.BlockSpec(memory_space=pl.ANY)] * 3 + [vmem] * 2,
        out_specs=(vmem, vmem),
        scratch_shapes=[
            pltpu.VMEM((T, rows, width), BF16),
            pltpu.VMEM((PAGE, T * width), BF16),
            pltpu.VMEM((rows, kvw), BF16),
            pltpu.VMEM((R + 1, rows, kvw), BF16),
            pltpu.VMEM((R, 16, rows), jnp.int32),
            pltpu.VMEM((T, rows, local_heads * HD), BF16),
            pltpu.VMEM((T, local_heads * HD, width), BF16),
            pltpu.VMEM((rows, 128), jnp.int32),
            pltpu.VMEM((2, local_heads, rows // 2, 1), F32),
            pltpu.VMEM((2, local_heads, rows // 2, 1), F32),
            pltpu.VMEM((2, local_heads, rows // 2, 128), F32),
            pltpu.VMEM(query_weight.shape, BF16),
            pltpu.VMEM(query_weight.shape, BF16),
            pltpu.VMEM(query_weight.shape, BF16),
            dma((3,)),
            dma((T, C)), dma((T, C)), dma((T, C)),
            dma((T,)), dma((T,)), dma((G,)), dma((G,)), dma((R,)), dma((R,)),
            dma((R + 1, C)), dma((R + 1, C)), dma((R + 1, C)), dma((T, 2)), dma((T, 2)),
        ],
        compiler_params=pltpu.CompilerParams(
            collective_id=0, has_side_effects=True, vmem_limit_bytes=56 * 1024 * 1024
        ),
        cost_estimate=pl.CostEstimate(flops=4 * 10**9, bytes_accessed=8 * 10**6, transcendentals=5 * 10**6),
    )(residual, norm_gain[None, :], freq_t, query_weight, key_weight, value_weight, out_weight, meta_t)
    return hidden, cache


def solution(mesh):
    return jax.shard_map(
        functools.partial(body, mesh.shape["seq"], mesh.shape["tp"]),
        mesh=mesh,
        in_specs=(
            P("seq", "tp"),
            P(),
            P(None, "tp"),
            P(None, "tp"),
            P(None, "tp"),
            P("tp", None),
            P("seq"),
            P("seq"),
            P("seq"),
        ),
        out_specs=(P("seq", "tp"), P("seq", None, "tp")),
        check_vma=False,
    )
```
